512 devices in a mesh: dp: 32 (over x, z_lo, core), ffn: 16 (over y, z_hi).
Axes of the slice: x: 4, y: 8, z: 8 (z_hi: 2, z_lo: 4; z = z_hi * 4 + z_lo), core: 2. Of those that a mesh axis runs over, the one named last changes fastest.
Arguments:
- train_act: bfloat16 [16384, 25600], P('dp', 'ffn'), may hold values from -6 to 6
- train_grad: bfloat16 [16384, 5120], P('dp', 'ffn'), may hold values from -6 to 6
- train_seg: int32 [32, 512], P('dp'), may hold values from 0 to 3, never falling along the last dimension, each value on 1 to 256 neighbouring positions
- train_mask: int32 [32, 512], P('dp'), may hold values 0 or 1
- test_act: bfloat16 [1024, 25600], P('dp', 'ffn'), may hold values from -6 to 6
- test_grad: bfloat16 [1024, 5120], P('dp', 'ffn'), may hold values from -6 to 6
- test_seg: int32 [1024], replicated, may hold values from 0 to 7, never falling along the last dimension, each value on 1 to 256 neighbouring positions
- test_mask: int32 [1024], replicated, may hold values 0 or 1
Outputs:
- scores: float32 [128, 8], P('dp')
The draws below stay inside these ranges and needn't reach their ends.
Inputs may be any that keep to these rules, and one draw needn't show every extreme that they name: `train_seg`: each block holds 4 sequences of 1 to 256 tokens in order, one of exactly 256. `test_seg`: sequences in order, each 1 to 256 tokens, one of exactly 256.
All inputs are finite; a program needn't handle non-finite values. No bound on the sum of `train_mask` on one device may be relied on, other than what follows from the above.
Results may differ from the reference program's by a relative error of at most 0.0003.
Values may be sent and summed in bfloat16 or wider, within the bound.
No kernel may reach another device: no remote copies, remote signals or barrier semaphores. Data moves between devices by JAX's collectives and lax.ppermute only.
A program may use at most 64 MiB of HBM per device.

```python
import math
import jax
import jax.numpy as jnp
import numpy as np
from jax import lax

D = 5120
FF = 25600
SEG_LEN = 256
SEQ_PACK = 4
PACK_LEN = 512
TEST_TOK = 1024
TEST_SEQS = 8
PACKS = 32
TRAIN_SEQS = 128


def set_ends(drawn, key, least, high):
    spot = [jax.random.randint(jax.random.fold_in(key, axis), (), 0, length) for axis, length in enumerate(drawn.shape)]
    longest = drawn.shape.index(max(drawn.shape))
    neighbour = spot[:longest] + [(spot[longest] + 1) % drawn.shape[longest]] + spot[longest + 1:]
    return drawn.at[tuple(spot)].set(least).at[tuple(neighbour)].set(high)


def steps_of(stream_key, dims, shards, low, high):
    def one(axis_at, parts):
        steps = jax.random.uniform(jax.random.fold_in(jax.random.fold_in(stream_key, 6), axis_at), (parts,), jnp.float32, low / len(shards), high / len(shards))
        return jnp.repeat(jnp.exp(steps), dims[axis_at] // parts).reshape((-1,) + (1,) * (len(dims) - axis_at - 1))

    level = one(*shards[0])
    for cut in shards[1:]:
        level = level * one(*cut)
    return level


def length_profile(amount, total, limit, lean):
    portions = [(1 << 20) // math.isqrt(standing ** lean) + 1 for standing in range(2, amount + 1)]
    surplus, holding = total - limit - (amount - 1), [1] * (amount - 1)
    while surplus > 0:
        candidates = [i for i in range(amount - 1) if holding[i] < limit]
        pool, remaining = sum([portions[i] for i in candidates]), surplus
        for i in candidates:
            addition = min(limit - holding[i], max(1, remaining * portions[i] // pool), surplus)
            holding[i] = holding[i] + addition
            surplus = surplus - addition
    return np.array([limit] + holding)


def ragged(rng, amount, total, reach, slope):
    if amount == 2:
        one = jax.random.randint(rng, (), max(1, total - reach), min(reach, total - 1) + 1)
        return jnp.stack([one, total - one])
    lengths = jnp.asarray(length_profile(amount, total, reach, slope), jnp.int32)
    twos = (amount - 1) // 2
    donor, sink = lengths[1:1 + 2 * twos:2], lengths[2:2 + 2 * twos:2]
    slack = jnp.minimum(donor - 1, reach - sink)
    passed = jax.random.randint(jax.random.fold_in(rng, 1), (twos,), 0, 1 << 20) % (slack + 1)
    lengths = lengths.at[1:1 + 2 * twos:2].set(donor - passed).at[2:2 + 2 * twos:2].set(sink + passed)
    return lengths[jax.random.permutation(jax.random.fold_in(rng, 2), amount)]


def bell_draw(key, shape, scale, limit, pieces=(), held_as=jnp.bfloat16):
    loudness = steps_of(key, shape, pieces, -0.22, 0.18) if pieces else 1.0
    drawn = jax.random.normal(key, shape, jnp.float32) * scale * loudness
    return jnp.minimum(jnp.maximum(drawn, -limit), limit).astype(held_as)


def setup_inputs(seed: int = 0) -> dict:
    keys = jax.random.split(jax.random.key(seed), 9)
    return {
        "train_act": bell_draw(keys[0], (PACKS * PACK_LEN, FF), 1.0, 6.0, ((0, 32), (1, 16))),
        "train_grad": bell_draw(keys[1], (PACKS * PACK_LEN, D), 1.0, 6.0, ((0, 32), (1, 16))),
        "train_seg": jax.vmap(lambda own: jnp.searchsorted(jnp.cumsum(ragged(own, SEQ_PACK, PACK_LEN, SEG_LEN, 2)), jnp.arange(PACK_LEN), side="right"))(jax.random.split(keys[2], PACKS)).reshape((PACKS, PACK_LEN)).astype(jnp.int32),
        "train_mask": set_ends((jax.random.randint(keys[3], (PACKS, PACK_LEN), 0, 4) < 3).astype(jnp.int32), jax.random.fold_in(keys[3], 1), 0, 1),
        "test_act": bell_draw(keys[4], (TEST_TOK, FF), 1.0, 6.0, ((0, 32), (1, 16))),
        "test_grad": bell_draw(keys[5], (TEST_TOK, D), 1.0, 6.0, ((0, 32), (1, 16))),
        "test_seg": jnp.searchsorted(jnp.cumsum(ragged(keys[6], TEST_SEQS, TEST_TOK, SEG_LEN, 2)), jnp.arange(TEST_TOK), side="right").astype(jnp.int32),
        "test_mask": set_ends((jax.random.randint(keys[7], (TEST_TOK,), 0, 4) < 3).astype(jnp.int32), jax.random.fold_in(keys[7], 1), 0, 1),
    }


def reference(train_act, train_grad, train_seg, train_mask, test_act, test_grad, test_seg, test_mask):
    masked_train = train_grad * train_mask.reshape(-1, 1).astype(jnp.bfloat16)
    masked_test = test_grad * test_mask.reshape(-1, 1).astype(jnp.bfloat16)
    act_gram = jnp.dot(train_act, test_act.T, preferred_element_type=jnp.float32)
    grad_gram = jnp.dot(masked_train, masked_test.T, preferred_element_type=jnp.float32)
    joint = act_gram * grad_gram
    block_ids = jnp.arange(train_seg.shape[0], dtype=jnp.int32).reshape(-1, 1) * SEQ_PACK
    train_ids = (train_seg + block_ids).reshape(-1)
    train_onehot = (train_ids[None, :] == jnp.arange(TRAIN_SEQS, dtype=jnp.int32)[:, None]).astype(jnp.float32)
    test_onehot = (test_seg[:, None] == jnp.arange(TEST_SEQS, dtype=jnp.int32)[None, :]).astype(jnp.float32)
    per_train = jnp.dot(train_onehot, joint, precision=lax.Precision.HIGHEST)
    scores = jnp.dot(per_train, test_onehot, precision=lax.Precision.HIGHEST)
    return scores / (SEG_LEN * math.sqrt(FF * D))
```

```python
import math

import jax
import jax.numpy as jnp
from jax import lax
from jax.sharding import Mesh, PartitionSpec as P

D = 5120
FF = 25600
SEG_LEN = 256
SEQ_PACK = 4
TEST_SEQS = 8
NX, NZ, NC, NY, NH = 4, 4, 2, 8, 2
DP = ("x", "z", "c")
FFN = ("y", "h")


def cross_rows(left, right):
    return lax.dot_general(
        left, right, (((1,), (1,)), ((), ())), preferred_element_type=jnp.float32
    )


def swap(value, axis):
    return lax.ppermute(value, axis, [(0, 1), (1, 0)])


def over_x(value):
    return [value] + [
        lax.ppermute(value, "x", [(i, (i + step) % NX) for i in range(NX)]) for step in (1, 3, 2)
    ]


def on_device(
    train_act, train_grad, train_seg, train_mask, test_act, test_grad, test_seg, test_mask
):
    x, y, h, c = (lax.axis_index(a) for a in ("x", "y", "h", "c"))
    grad_z = lax.all_gather(test_grad, "z", axis=0, tiled=True)
    act_z = lax.all_gather(test_act, "z", axis=0, tiled=True)
    other_grad, other_act = swap(train_grad, "c"), swap(train_act, "c")
    grads = over_x(grad_z)
    acts = over_x(act_z)

    def gram(chunks, own, other):
        both = jnp.concatenate([own, other], 0)
        return jnp.concatenate([cross_rows(t, both) for t in chunks], 0)

    grad_gram = gram(grads, train_grad, other_grad)
    grad_part = lax.psum_scatter(grad_gram, "y", scatter_dimension=0, tiled=True)
    act_gram = gram(acts, train_act, other_act)
    act_part = lax.psum_scatter(act_gram, "y", scatter_dimension=0, tiled=True)

    half = act_part.shape[0] // 2

    def over_h(part):
        keep = lax.dynamic_slice_in_dim(part, h * half, half, 0)
        send = lax.dynamic_slice_in_dim(part, (1 - h) * half, half, 0)
        return keep + swap(send, "h")

    joint = over_h(act_part) * over_h(grad_part)
    behind = (y // 2) ^ (y // 4)
    first = (((x - behind) % NX * NZ + 2 * (y % 2) + h) * NC + c) * half
    seg = lax.dynamic_slice_in_dim(test_seg, first, half, 0)
    mask = lax.dynamic_slice_in_dim(test_mask, first, half, 0)
    test_onehot = (
        (seg[None, :] == jnp.arange(TEST_SEQS, dtype=jnp.int32)[:, None]) & (mask != 0)[None, :]
    ).astype(jnp.float32)
    rows = jnp.dot(test_onehot, joint, precision=lax.Precision.HIGHEST)
    n = train_act.shape[0]
    mine, theirs = rows[:, :n], rows[:, n:]
    ordered = jnp.where(
        c == 0, jnp.concatenate([mine, theirs], 1), jnp.concatenate([theirs, mine], 1)
    )
    total = lax.psum(ordered, ("y", "c"))
    total = lax.dynamic_slice_in_dim(total, c * n, n, 1)
    total = total + swap(total, "h")
    train_onehot = (
        (train_seg == jnp.arange(SEQ_PACK, dtype=jnp.int32)[:, None]) & (train_mask != 0)
    ).astype(jnp.float32)
    scores = lax.dot_general(
        train_onehot, total, (((1,), (1,)), ((), ())), precision=lax.Precision.HIGHEST
    )
    return scores * (1.0 / (SEG_LEN * math.sqrt(FF * D)))


def solution(mesh):
    fine = Mesh(mesh.devices.reshape(NX, NZ, NC, NY, NH), ("x", "z", "c", "y", "h"))
    return jax.shard_map(
        on_device,
        mesh=fine,
        in_specs=(P(DP, FFN), P(DP, FFN), P(DP, None), P(DP, None), P(DP, FFN), P(DP, FFN), P(), P()),
        out_specs=P(DP, None),
        check_vma=False,
    )
```

```python
import math

import jax
import jax.numpy as jnp
from jax import lax
from jax.sharding import Mesh, PartitionSpec as P

D = 5120
FF = 25600
SEG_LEN = 256
SEQ_PACK = 4
TEST_SEQS = 8
NX, NZ, NC, NY, NH = 4, 4, 2, 8, 2
DP = ("x", "z", "c")
FFN = ("y", "h")


def cross_rows(left, right):
    return lax.dot_general(
        left, right, (((1,), (1,)), ((), ())), preferred_element_type=jnp.float32
    )


def swap(value, axis):
    return lax.ppermute(value, axis, [(0, 1), (1, 0)])


def over_x(value):
    return [value] + [
        lax.ppermute(value, "x", [(i, (i + step) % NX) for i in range(NX)]) for step in (1, 3, 2)
    ]


def on_device(
    train_act, train_grad, train_seg, train_mask, test_act, test_grad, test_seg, test_mask
):
    x, y, h, c = (lax.axis_index(a) for a in ("x", "y", "h", "c"))
    wide = test_act.shape[1]
    both_z = lax.all_gather(jnp.concatenate([test_act, test_grad], 1), "z", axis=0, tiled=True)
    act_z, grad_z = both_z[:, :wide], both_z[:, wide:]
    other_grad, other_act = swap(train_grad, "c"), swap(train_act, "c")
    grads = over_x(grad_z)
    acts = over_x(act_z)

    def gram(chunks, own, other):
        both = jnp.concatenate([own, other], 0)
        return jnp.concatenate([cross_rows(t, both) for t in chunks], 0)

    grad_gram = gram(grads, train_grad, other_grad)
    grad_part = lax.psum_scatter(grad_gram, "y", scatter_dimension=0, tiled=True)
    act_gram = gram(acts, train_act, other_act)
    act_part = lax.psum_scatter(act_gram, "y", scatter_dimension=0, tiled=True)

    half = act_part.shape[0] // 2

    def over_h(part):
        keep = lax.dynamic_slice_in_dim(part, h * half, half, 0)
        send = lax.dynamic_slice_in_dim(part, (1 - h) * half, half, 0)
        return keep + swap(send, "h")

    joint = over_h(act_part) * over_h(grad_part)
    behind = (y // 2) ^ (y // 4)
    first = (((x - behind) % NX * NZ + 2 * (y % 2) + h) * NC + c) * half
    seg = lax.dynamic_slice_in_dim(test_seg, first, half, 0)
    mask = lax.dynamic_slice_in_dim(test_mask, first, half, 0)
    test_onehot = (
        (seg[None, :] == jnp.arange(TEST_SEQS, dtype=jnp.int32)[:, None]) & (mask != 0)[None, :]
    ).astype(jnp.float32)
    rows = jnp.dot(test_onehot, joint, precision=lax.Precision.HIGHEST)
    n = train_act.shape[0]
    mine, theirs = rows[:, :n], rows[:, n:]
    total = mine + swap(theirs, "c")
    train_onehot = (
        (train_seg == jnp.arange(SEQ_PACK, dtype=jnp.int32)[:, None]) & (train_mask != 0)
    ).astype(jnp.float32)
    scores = lax.dot_general(
        train_onehot, total, (((1,), (1,)), ((), ())), precision=lax.Precision.HIGHEST
    )
    scores = lax.psum(scores, "y")
    scores = scores + swap(scores, "h")
    return scores * (1.0 / (SEG_LEN * math.sqrt(FF * D)))


def solution(mesh):
    fine = Mesh(mesh.devices.reshape(NX, NZ, NC, NY, NH), ("x", "z", "c", "y", "h"))
    return jax.shard_map(
        on_device,
        mesh=fine,
        in_specs=(P(DP, FFN), P(DP, FFN), P(DP, None), P(DP, None), P(DP, FFN), P(DP, FFN), P(), P()),
        out_specs=P(DP, None),
        check_vma=False,
    )
```

```python
import math

import jax
import jax.numpy as jnp
from jax import lax
from jax.experimental import pallas as pl
from jax.experimental.pallas import tpu as pltpu
from jax.sharding import Mesh, PartitionSpec as P

D = 5120
FF = 25600
SEG_LEN = 256
SEQ_PACK = 4
TEST_SEQS = 8
NX, NZ, NC, NY, NH = 4, 4, 2, 8, 2
DP = ("x", "z", "c")
FFN = ("y", "h")
LANES = 128
SCALE_ROWS = 16
STEPS = 128.0
TOP = 32000.0


def cross_rows(left, right):
    return lax.dot_general(
        left, right, (((1,), (1,)), ((), ())), preferred_element_type=jnp.float32
    )


def swap(value, axis):
    return lax.ppermute(value, axis, [(0, 1), (1, 0)])


def over_x(value):
    return [value] + [
        lax.ppermute(value, "x", [(i, (i + step) % NX) for i in range(NX)]) for step in (1, 3, 2)
    ]


def pack_kernel(*refs):
    chunks, out = refs[:-1], refs[-1]
    rows = chunks[0].shape[0] * len(chunks) // NY
    blocks = chunks[0].shape[1] // LANES
    exponents = []
    for b in range(blocks):
        cols = slice(b * LANES, (b + 1) * LANES)
        parts = [r[:, cols] for r in chunks]
        most = jnp.max(jnp.abs(parts[0]), axis=0, keepdims=True)
        for p in parts[1:]:
            most = jnp.maximum(most, jnp.max(jnp.abs(p), axis=0, keepdims=True))
        e = jnp.ceil(jnp.log(jnp.maximum(most, 1e-30)) * STEPS)
        factor = jnp.exp(e * (-1.0 / STEPS)) * TOP
        exponents.append(e)
        for d in range(NY):
            per = chunks[0].shape[0] // rows
            p = parts[d // per][(d % per) * rows : (d % per + 1) * rows]
            q = jnp.round(p * factor).astype(jnp.int32).astype(jnp.int16)
            out[d, b * rows : (b + 1) * rows, :] = q
    pad = [jnp.zeros((SCALE_ROWS - blocks, LANES), jnp.float32)]
    tail = jnp.concatenate(exponents + pad, 0).astype(jnp.int32).astype(jnp.int16)
    for d in range(NY):
        out[d, blocks * rows : blocks * rows + SCALE_ROWS, :] = tail


def unpack_kernel(h_ref, got, keep, send):
    half = keep.shape[0]
    rows = 2 * half
    blocks = keep.shape[1] // LANES
    mine = h_ref[0] == 0
    factors = []
    for s in range(NY):
        e = got[s, blocks * rows : blocks * rows + SCALE_ROWS, :].astype(jnp.float32)
        factors.append(jnp.exp(e * (1.0 / STEPS)) * (1.0 / TOP))
    for b in range(blocks):
        cols = slice(b * LANES, (b + 1) * LANES)
        total = jnp.zeros((rows, LANES), jnp.float32)
        for s in range(NY):
            block = got[s, b * rows : (b + 1) * rows, :].astype(jnp.float32)
            total = total + block * factors[s][b : b + 1]
        low, high = total[:half], total[half:]
        keep[:, cols] = jnp.where(mine, low, high)
        send[:, cols] = jnp.where(mine, high, low)


def sum_over_y(chunks, h):
    tokens = chunks[0].shape[1]
    rows = chunks[0].shape[0] * len(chunks) // NY
    packed = pl.pallas_call(
        pack_kernel,
        out_shape=jax.ShapeDtypeStruct(
            (NY, tokens // LANES * rows + SCALE_ROWS, LANES), jnp.int16
        ),
        in_specs=[pl.BlockSpec(memory_space=pltpu.VMEM)] * len(chunks),
        out_specs=pl.BlockSpec(memory_space=pltpu.VMEM),
        compiler_params=pltpu.CompilerParams(vmem_limit_bytes=24 << 20),
    )(*chunks)
    got = lax.all_to_all(packed, "y", 0, 0, tiled=True)
    half = jax.ShapeDtypeStruct((rows // 2, tokens), jnp.float32)
    return pl.pallas_call(
        unpack_kernel,
        out_shape=(half, half),
        in_specs=[
            pl.BlockSpec(memory_space=pltpu.SMEM),
            pl.BlockSpec(memory_space=pltpu.VMEM),
        ],
        out_specs=(pl.BlockSpec(memory_space=pltpu.VMEM),) * 2,
        compiler_params=pltpu.CompilerParams(vmem_limit_bytes=24 << 20),
    )(h.reshape(1), got)


def on_device(
    train_act, train_grad, train_seg, train_mask, test_act, test_grad, test_seg, test_mask
):
    x, y, h, c = (lax.axis_index(a) for a in ("x", "y", "h", "c"))
    wide = test_act.shape[1]
    both_z = lax.all_gather(jnp.concatenate([test_act, test_grad], 1), "z", axis=0, tiled=True)
    act_z, grad_z = both_z[:, :wide], both_z[:, wide:]
    other_grad, other_act = swap(train_grad, "c"), swap(train_act, "c")
    grads = over_x(grad_z)
    acts = over_x(act_z)

    def grams(chunks, own, other):
        both = jnp.concatenate([own, other], 0)
        return [cross_rows(t, both) for t in chunks]

    grad_gram = jnp.concatenate(grams(grads, train_grad, other_grad), 0)
    grad_part = lax.psum_scatter(grad_gram, "y", scatter_dimension=0, tiled=True)
    act_keep, act_send = sum_over_y(grams(acts, train_act, other_act), h)

    half = act_keep.shape[0]
    grad_keep = lax.dynamic_slice_in_dim(grad_part, h * half, half, 0)
    grad_send = lax.dynamic_slice_in_dim(grad_part, (1 - h) * half, half, 0)
    joint = (act_keep + swap(act_send, "h")) * (grad_keep + swap(grad_send, "h"))
    behind = (y // 2) ^ (y // 4)
    first = (((x - behind) % NX * NZ + 2 * (y % 2) + h) * NC + c) * half
    seg = lax.dynamic_slice_in_dim(test_seg, first, half, 0)
    mask = lax.dynamic_slice_in_dim(test_mask, first, half, 0)
    test_onehot = (
        (seg[None, :] == jnp.arange(TEST_SEQS, dtype=jnp.int32)[:, None]) & (mask != 0)[None, :]
    ).astype(jnp.float32)
    rows = jnp.dot(test_onehot, joint, precision=lax.Precision.HIGHEST)
    n = train_act.shape[0]
    mine, theirs = rows[:, :n], rows[:, n:]
    total = mine + swap(theirs, "c")
    train_onehot = (
        (train_seg == jnp.arange(SEQ_PACK, dtype=jnp.int32)[:, None]) & (train_mask != 0)
    ).astype(jnp.float32)
    scores = lax.dot_general(
        train_onehot, total, (((1,), (1,)), ((), ())), precision=lax.Precision.HIGHEST
    )
    scores = lax.psum(scores, "y")
    scores = scores + swap(scores, "h")
    return scores * (1.0 / (SEG_LEN * math.sqrt(FF * D)))


def solution(mesh):
    fine = Mesh(mesh.devices.reshape(NX, NZ, NC, NY, NH), ("x", "z", "c", "y", "h"))
    return jax.shard_map(
        on_device,
        mesh=fine,
        in_specs=(P(DP, FFN), P(DP, FFN), P(DP, None), P(DP, None), P(DP, FFN), P(DP, FFN), P(), P()),
        out_specs=P(DP, None),
        check_vma=False,
    )
```

```python
import math

import jax
import jax.numpy as jnp
from jax import lax
from jax.experimental import pallas as pl
from jax.experimental.pallas import tpu as pltpu
from jax.sharding import Mesh, PartitionSpec as P

D = 5120
FF = 25600
SEG_LEN = 256
SEQ_PACK = 4
TEST_SEQS = 8
NX, NZ, NC, NY, NH = 4, 4, 2, 8, 2
DP = ("x", "z", "c")
FFN = ("y", "h")
LANES = 128
BLOCKS = 8
SCALE_ROWS = 16
STEPS = 128.0
TOP = 32000.0


def cross_rows(left, right):
    return lax.dot_general(
        left, right, (((1,), (1,)), ((), ())), preferred_element_type=jnp.float32
    )


def swap(value, axis):
    return lax.ppermute(value, axis, [(0, 1), (1, 0)])


def over_x(value):
    return [value] + [
        lax.ppermute(value, "x", [(i, (i + step) % NX) for i in range(NX)]) for step in (1, 3, 2)
    ]


def pack(parts, out, lead):
    blocks = parts.blocks
    exponents = []
    for b in range(blocks):
        pieces = parts(b)
        rows = pieces[0].shape[0]
        most = jnp.max(jnp.abs(pieces[0]), axis=0, keepdims=True)
        for p in pieces[1:]:
            most = jnp.maximum(most, jnp.max(jnp.abs(p), axis=0, keepdims=True))
        e = jnp.ceil(jnp.log(jnp.maximum(most, 1e-30)) * STEPS)
        factor = jnp.exp(e * (-1.0 / STEPS)) * TOP
        exponents.append(e)
        for i, p in enumerate(pieces):
            q = jnp.round(p * factor).astype(jnp.int32).astype(jnp.int16)
            out[lead[i] + (slice(b * rows, (b + 1) * rows), slice(None))] = q
    pad = [jnp.zeros((SCALE_ROWS - blocks, LANES), jnp.float32)]
    tail = jnp.concatenate(exponents + pad, 0).astype(jnp.int32).astype(jnp.int16)
    for at in lead:
        out[at + (slice(blocks * rows, blocks * rows + SCALE_ROWS), slice(None))] = tail


class Pieces:
    def __init__(self, blocks, get):
        self.blocks, self.get = blocks, get

    def __call__(self, b):
        return self.get(b)


def factors_of(tail):
    return jnp.exp(tail.astype(jnp.float32) * (1.0 / STEPS)) * (1.0 / TOP)


def pack_kernel(*refs):
    chunks, out = refs[:-1], refs[-1]
    rows = chunks[0].shape[0] * len(chunks) // NY
    per = chunks[0].shape[0] // rows

    def pieces(b):
        cols = slice(b * LANES, (b + 1) * LANES)
        return [
            chunks[d // per][(d % per) * rows : (d % per + 1) * rows, cols] for d in range(NY)
        ]

    pack(Pieces(chunks[0].shape[1] // LANES, pieces), out, [(d,) for d in range(NY)])


def unpack_kernel(got, out):
    blocks = BLOCKS
    rows = (got.shape[1] - SCALE_ROWS) // blocks
    factors = [factors_of(got[s, blocks * rows :, :]) for s in range(NY)]

    def pieces(b):
        total = jnp.zeros((rows, LANES), jnp.float32)
        for s in range(NY):
            block = got[s, b * rows : (b + 1) * rows, :].astype(jnp.float32)
            total = total + block * factors[s][b : b + 1]
        return [total]

    pack(Pieces(blocks, pieces), out, [()])


def joint_kernel(onehot, act_own, act_other, grad_own, grad_other, out):
    blocks = BLOCKS
    rows = (act_own.shape[0] - SCALE_ROWS) // blocks

    def part(ref, factor, b):
        return ref[b * rows : (b + 1) * rows, :].astype(jnp.float32) * factor[b : b + 1]

    refs = (act_own, act_other, grad_own, grad_other)
    f = [factors_of(r[blocks * rows :, :]) for r in refs]
    for b in range(blocks):
        a0, a1, g0, g1 = (part(r, k, b) for r, k in zip(refs, f))
        joint = (a0 + a1) * (g0 + g1)
        out[:, b * LANES : (b + 1) * LANES] = lax.dot_general(
            onehot[...],
            joint,
            (((1,), (0,)), ((), ())),
            precision=lax.Precision.HIGHEST,
            preferred_element_type=jnp.float32,
        )


VMEM = pl.BlockSpec(memory_space=pltpu.VMEM)


def call(kernel, shape, dtype, *args):
    return pl.pallas_call(
        kernel,
        out_shape=jax.ShapeDtypeStruct(shape, dtype),
        in_specs=[VMEM] * len(args),
        out_specs=VMEM,
        compiler_params=pltpu.CompilerParams(vmem_limit_bytes=24 << 20),
    )(*args)


def sum_over_y(chunks):
    rows = chunks[0].shape[0] * len(chunks) // NY
    height = BLOCKS * rows + SCALE_ROWS
    packed = call(pack_kernel, (NY, height, LANES), jnp.int16, *chunks)
    got = lax.all_to_all(packed, "y", 0, 0, tiled=True)
    return call(unpack_kernel, (height, LANES), jnp.int16, got)


def on_device(
    train_act, train_grad, train_seg, train_mask, test_act, test_grad, test_seg, test_mask
):
    x, y, c = (lax.axis_index(a) for a in ("x", "y", "c"))
    wide = test_act.shape[1]
    both_z = lax.all_gather(jnp.concatenate([test_act, test_grad], 1), "z", axis=0, tiled=True)
    act_z, grad_z = both_z[:, :wide], both_z[:, wide:]
    other_grad, other_act = swap(train_grad, "c"), swap(train_act, "c")
    grads = over_x(grad_z)
    acts = over_x(act_z)

    def grams(chunks, own, other):
        both = jnp.concatenate([own, other], 0)
        return [cross_rows(t, both) for t in chunks]

    grad_y = sum_over_y(grams(grads, train_grad, other_grad))
    act_y = sum_over_y(grams(acts, train_act, other_act))
    behind = (y // 2) ^ (y // 4)
    local = test_act.shape[0]
    seg, mask = (
        lax.dynamic_slice(
            v.reshape(NX, NZ, NC, local), ((x - behind) % NX, 2 * (y % 2), c, 0), (1, 2, 1, local)
        ).reshape(1, -1)
        for v in (test_seg, test_mask)
    )
    test_onehot = (
        (seg == jnp.arange(TEST_SEQS, dtype=jnp.int32)[:, None]) & (mask != 0)
    ).astype(jnp.float32)
    grad_other, act_other = swap(grad_y, "h"), swap(act_y, "h")
    rows = call(
        joint_kernel,
        (TEST_SEQS, BLOCKS * LANES),
        jnp.float32,
        test_onehot,
        act_y,
        act_other,
        grad_y,
        grad_other,
    )
    n = train_act.shape[0]
    mine, theirs = rows[:, :n], rows[:, n:]
    total = mine + swap(theirs, "c")
    train_onehot = (
        (train_seg == jnp.arange(SEQ_PACK, dtype=jnp.int32)[:, None]) & (train_mask != 0)
    ).astype(jnp.float32)
    scores = lax.dot_general(
        train_onehot, total, (((1,), (1,)), ((), ())), precision=lax.Precision.HIGHEST
    )
    scores = lax.psum(scores, "y")
    return scores * (1.0 / (SEG_LEN * math.sqrt(FF * D)))


def solution(mesh):
    fine = Mesh(mesh.devices.reshape(NX, NZ, NC, NY, NH), ("x", "z", "c", "y", "h"))
    return jax.shard_map(
        on_device,
        mesh=fine,
        in_specs=(P(DP, FFN), P(DP, FFN), P(DP, None), P(DP, None), P(DP, FFN), P(DP, FFN), P(), P()),
        out_specs=P(DP, None),
        check_vma=False,
    )
```

```python
import math

import jax
import jax.numpy as jnp
from jax import lax
from jax.experimental import pallas as pl
from jax.experimental.pallas import tpu as pltpu
from jax.sharding import Mesh, PartitionSpec as P

D = 5120
FF = 25600
SEG_LEN = 256
SEQ_PACK = 4
TEST_SEQS = 8
NX, NZ, NC, NY, NH = 4, 4, 2, 8, 2
DP = ("x", "z", "c")
FFN = ("y", "h")
LANES = 128
BLOCKS = 8
SCALE_ROWS = 16
STEPS = 128.0
TOP = 32000.0


def swap(value, axis):
    return lax.ppermute(value, axis, [(0, 1), (1, 0)])


ORDER = (3, 1, 2)


def around(value, axis):
    return [lax.ppermute(value, axis, [(i, (i + s) % 4) for i in range(4)]) for s in ORDER]


def behind(k):
    return jnp.where(k == 0, 0, jnp.where(k == 1, ORDER[0], jnp.where(k == 2, ORDER[1], ORDER[2])))


def scales(pieces):
    most = jnp.max(jnp.abs(pieces[0]), axis=0, keepdims=True)
    for p in pieces[1:]:
        most = jnp.maximum(most, jnp.max(jnp.abs(p), axis=0, keepdims=True))
    e = jnp.ceil(jnp.log(jnp.maximum(most, 1e-30)) * STEPS)
    return e, jnp.exp(e * (-1.0 / STEPS)) * TOP


def steps_of(value, factor):
    return jnp.round(value * factor).astype(jnp.int32).astype(jnp.int16)


def factors_of(tail):
    return jnp.exp(tail.astype(jnp.float32) * (1.0 / STEPS)) * (1.0 / TOP)


def tail_of(exponents):
    return jnp.concatenate(exponents, 0).astype(jnp.int32).astype(jnp.int16)


def gram_kernel(*refs):
    act, act_other, grad, grad_other = refs[-8:-4]
    out, low, a_gram, g_gram = refs[-4:]
    chunks = refs[:-8]
    wide, n = act.shape
    height = chunks[0].shape[0]
    base = wide // LANES * LANES
    low[: wide - base, :] = jnp.zeros((wide - base, 2 * n), jnp.bfloat16)
    low[wide - base :, :n] = grad[...]
    low[wide - base :, n:] = grad_other[...]
    for j, t in enumerate(chunks):
        rows = slice(j * height, (j + 1) * height)
        left = t[:, :wide]
        a_gram[rows, :n] = jnp.dot(left, act[...], preferred_element_type=jnp.float32)
        a_gram[rows, n:] = jnp.dot(left, act_other[...], preferred_element_type=jnp.float32)
        g_gram[rows, :] = jnp.dot(t[:, base:], low[...], preferred_element_type=jnp.float32)
    per = height // NY
    count = len(chunks)
    exponents = []
    for k, gram in enumerate((a_gram, g_gram)):
        for b in range(BLOCKS):
            cols = slice(b * LANES, (b + 1) * LANES)
            e, factor = scales([gram[:, cols]])
            exponents.append(e)
            for d in range(NY):
                for j in range(count):
                    top = (2 * b + k) * per * count + j * per
                    first = j * height + d * per
                    out[d, top : top + per, :] = steps_of(gram[first : first + per, cols], factor)
    tail = tail_of(exponents)
    for d in range(NY):
        out[d, 2 * BLOCKS * per * count :, :] = tail


def unpack_kernel(got, out):
    rows = (got.shape[1] - SCALE_ROWS) // (2 * BLOCKS)
    factors = [factors_of(got[s, 2 * BLOCKS * rows :, :]) for s in range(NY)]
    exponents = []
    for k in range(2):
        for b in range(BLOCKS):
            top = (2 * b + k) * rows
            at = k * BLOCKS + b
            total = jnp.zeros((rows, LANES), jnp.float32)
            for s in range(NY):
                block = got[s, top : top + rows, :].astype(jnp.float32)
                total = total + block * factors[s][at : at + 1]
            e, factor = scales([total])
            exponents.append(e)
            out[top : top + rows, :] = steps_of(total, factor)
    out[2 * BLOCKS * rows :, :] = tail_of(exponents)


def joint_kernel(*refs):
    out = refs[-1]
    groups = [refs[i : i + 3] for i in range(0, len(refs) - 1, 3)]
    totals = [0.0] * BLOCKS
    for onehot, own, other in groups:
        rows = (own.shape[0] - SCALE_ROWS) // (2 * BLOCKS)
        f_own = factors_of(own[2 * BLOCKS * rows :, :])
        f_other = factors_of(other[2 * BLOCKS * rows :, :])
        for b in range(BLOCKS):
            sums = []
            for k in range(2):
                top, at = (2 * b + k) * rows, k * BLOCKS + b
                sums.append(
                    own[top : top + rows, :].astype(jnp.float32) * f_own[at : at + 1]
                    + other[top : top + rows, :].astype(jnp.float32) * f_other[at : at + 1]
                )
            totals[b] = totals[b] + lax.dot_general(
                onehot[...],
                sums[0] * sums[1],
                (((1,), (0,)), ((), ())),
                precision=lax.Precision.HIGHEST,
                preferred_element_type=jnp.float32,
            )
    for b in range(BLOCKS):
        out[:, b * LANES : (b + 1) * LANES] = totals[b]


VMEM = pl.BlockSpec(memory_space=pltpu.VMEM)


def call(kernel, shape, dtype, *args, scratch=()):
    return pl.pallas_call(
        kernel,
        out_shape=jax.ShapeDtypeStruct(shape, dtype),
        in_specs=[VMEM] * len(args),
        out_specs=VMEM,
        scratch_shapes=list(scratch),
        compiler_params=pltpu.CompilerParams(vmem_limit_bytes=32 << 20),
    )(*args)


def sums_over_y(chunks, train):
    count = len(chunks)
    height, wide = chunks[0].shape[0], train[0].shape[0]
    tall = 2 * BLOCKS * (height // NY) * count + SCALE_ROWS
    base = wide // LANES * LANES
    tokens = 2 * train[0].shape[1]
    scratch = [
        pltpu.VMEM((chunks[0].shape[1] - base, tokens), jnp.bfloat16),
        pltpu.VMEM((count * height, tokens), jnp.float32),
        pltpu.VMEM((count * height, tokens), jnp.float32),
    ]
    packed = call(gram_kernel, (NY, tall, LANES), jnp.int16, *chunks, *train, scratch=scratch)
    got = lax.all_to_all(packed, "y", 0, 0, tiled=True)
    return call(unpack_kernel, (tall, LANES), jnp.int16, got)


def on_device(
    train_act, train_grad, train_seg, train_mask, test_act, test_grad, test_seg, test_mask
):
    x, y, z, c = (lax.axis_index(a) for a in ("x", "y", "z", "c"))
    own = jnp.concatenate([test_act, test_grad], 1)
    own = jnp.concatenate([own] + around(own, "z"), 0)
    act, grad = train_act.T, train_grad.T
    train = (act, swap(act, "c"), grad, swap(grad, "c"))
    others = around(own, "x")
    local = test_act.shape[0]
    per = own.shape[0] // NY
    packs = [sums_over_y([own], train), sums_over_y(others, train)]
    from_z = (z - behind(y * per // local)) % NZ

    def here(values):
        cut = lax.dynamic_slice(
            values.reshape(NX, NZ, NC, local), (0, from_z, c, y * per % local), (NX, 1, 1, per)
        ).reshape(NX, per)
        return [
            jnp.sum(jnp.where(jnp.arange(NX)[:, None] == (x - s) % NX, cut, 0), 0, keepdims=True)
            for s in (0,) + ORDER
        ]

    segs, masks = here(test_seg), here(test_mask)
    onehots = [
        ((seg == jnp.arange(TEST_SEQS, dtype=jnp.int32)[:, None]) & (mask != 0)).astype(jnp.float32)
        for seg, mask in zip(segs, masks)
    ]
    onehots = [onehots[0], jnp.concatenate(onehots[1:], 1)]
    args = []
    for onehot, pack in zip(onehots, packs):
        args += [onehot, pack, swap(pack, "h")]
    rows = call(joint_kernel, (TEST_SEQS, BLOCKS * LANES), jnp.float32, *args)
    n = train_act.shape[0]
    mine, theirs = rows[:, :n], rows[:, n:]
    total = mine + swap(theirs, "c")
    train_onehot = (
        (train_seg == jnp.arange(SEQ_PACK, dtype=jnp.int32)[:, None]) & (train_mask != 0)
    ).astype(jnp.float32)
    scores = lax.dot_general(
        train_onehot, total, (((1,), (1,)), ((), ())), precision=lax.Precision.HIGHEST
    )
    scores = lax.psum(scores, "y")
    return scores * (1.0 / (SEG_LEN * math.sqrt(FF * D)))


def solution(mesh):
    fine = Mesh(mesh.devices.reshape(NX, NZ, NC, NY, NH), ("x", "z", "c", "y", "h"))
    return jax.shard_map(
        on_device,
        mesh=fine,
        in_specs=(P(DP, FFN), P(DP, FFN), P(DP, None), P(DP, None), P(DP, FFN), P(DP, FFN), P(), P()),
        out_specs=P(DP, None),
        check_vma=False,
    )
```

```python
import math

import jax
import jax.numpy as jnp
from jax import lax
from jax.experimental import pallas as pl
from jax.experimental.pallas import tpu as pltpu
from jax.sharding import Mesh, PartitionSpec as P

D = 5120
FF = 25600
SEG_LEN = 256
SEQ_PACK = 4
TEST_SEQS = 8
NX, NZ, NC, NY, NH = 4, 4, 2, 8, 2
DP = ("x", "z", "c")
FFN = ("y", "h")
LANES = 128
BLOCKS = 8
SCALE_ROWS = 16
STEPS = 128.0
TOP = 32000.0


def cross_rows(left, right):
    return lax.dot_general(
        left, right, (((1,), (1,)), ((), ())), preferred_element_type=jnp.float32
    )


def swap(value, axis):
    return lax.ppermute(value, axis, [(0, 1), (1, 0)])


def over_x(value):
    return [value] + [
        lax.ppermute(value, "x", [(i, (i + step) % NX) for i in range(NX)]) for step in (1, 3, 2)
    ]


def pack(parts, out, lead):
    blocks = parts.blocks
    exponents = []
    for b in range(blocks):
        pieces = parts(b)
        rows = pieces[0].shape[0]
        most = jnp.max(jnp.abs(pieces[0]), axis=0, keepdims=True)
        for p in pieces[1:]:
            most = jnp.maximum(most, jnp.max(jnp.abs(p), axis=0, keepdims=True))
        e = jnp.ceil(jnp.log(jnp.maximum(most, 1e-30)) * STEPS)
        factor = jnp.exp(e * (-1.0 / STEPS)) * TOP
        exponents.append(e)
        for i, p in enumerate(pieces):
            q = jnp.round(p * factor).astype(jnp.int32).astype(jnp.int16)
            out[lead[i] + (slice(b * rows, (b + 1) * rows), slice(None))] = q
    pad = [jnp.zeros((SCALE_ROWS - blocks, LANES), jnp.float32)]
    tail = jnp.concatenate(exponents + pad, 0).astype(jnp.int32).astype(jnp.int16)
    for at in lead:
        out[at + (slice(blocks * rows, blocks * rows + SCALE_ROWS), slice(None))] = tail


class Pieces:
    def __init__(self, blocks, get):
        self.blocks, self.get = blocks, get

    def __call__(self, b):
        return self.get(b)


def factors_of(tail):
    return jnp.exp(tail.astype(jnp.float32) * (1.0 / STEPS)) * (1.0 / TOP)


def pack_kernel(*refs):
    chunks, out = refs[:-1], refs[-1]
    rows = chunks[0].shape[0] * len(chunks) // NY
    per = chunks[0].shape[0] // rows

    def pieces(b):
        cols = slice(b * LANES, (b + 1) * LANES)
        return [
            chunks[d // per][(d % per) * rows : (d % per + 1) * rows, cols] for d in range(NY)
        ]

    pack(Pieces(chunks[0].shape[1] // LANES, pieces), out, [(d,) for d in range(NY)])


def grad_kernel(order, test, own, other, out, gram):
    n = own.shape[1]
    gram[:, :n] = jnp.dot(test[...], own[...], preferred_element_type=jnp.float32)
    gram[:, n:] = jnp.dot(test[...], other[...], preferred_element_type=jnp.float32)
    height = test.shape[0] // NX
    rows = test.shape[0] // NY
    per = height // rows

    def pieces(b):
        cols = slice(b * LANES, (b + 1) * LANES)
        found = []
        for d in range(NY):
            first = pl.multiple_of(order[d // per] * height + (d % per) * rows, rows)
            found.append(gram[pl.ds(first, rows), cols])
        return found

    pack(Pieces(2 * n // LANES, pieces), out, [(d,) for d in range(NY)])


def unpack_kernel(got, out):
    blocks = BLOCKS
    rows = (got.shape[1] - SCALE_ROWS) // blocks
    factors = [factors_of(got[s, blocks * rows :, :]) for s in range(NY)]

    def pieces(b):
        total = jnp.zeros((rows, LANES), jnp.float32)
        for s in range(NY):
            block = got[s, b * rows : (b + 1) * rows, :].astype(jnp.float32)
            total = total + block * factors[s][b : b + 1]
        return [total]

    pack(Pieces(blocks, pieces), out, [()])


def joint_kernel(onehot, act_own, act_other, grad_own, grad_other, out):
    blocks = BLOCKS
    rows = (act_own.shape[0] - SCALE_ROWS) // blocks

    def part(ref, factor, b):
        return ref[b * rows : (b + 1) * rows, :].astype(jnp.float32) * factor[b : b + 1]

    refs = (act_own, act_other, grad_own, grad_other)
    f = [factors_of(r[blocks * rows :, :]) for r in refs]
    for b in range(blocks):
        a0, a1, g0, g1 = (part(r, k, b) for r, k in zip(refs, f))
        joint = (a0 + a1) * (g0 + g1)
        out[:, b * LANES : (b + 1) * LANES] = lax.dot_general(
            onehot[...],
            joint,
            (((1,), (0,)), ((), ())),
            precision=lax.Precision.HIGHEST,
            preferred_element_type=jnp.float32,
        )


VMEM = pl.BlockSpec(memory_space=pltpu.VMEM)


def call(kernel, shape, dtype, *args):
    return pl.pallas_call(
        kernel,
        out_shape=jax.ShapeDtypeStruct(shape, dtype),
        in_specs=[VMEM] * len(args),
        out_specs=VMEM,
        compiler_params=pltpu.CompilerParams(vmem_limit_bytes=24 << 20),
    )(*args)


def sum_over_y(packed):
    got = lax.all_to_all(packed, "y", 0, 0, tiled=True)
    return call(unpack_kernel, packed.shape[1:], jnp.int16, got)


def pack_acts(chunks):
    rows = chunks[0].shape[0] * len(chunks) // NY
    return call(pack_kernel, (NY, BLOCKS * rows + SCALE_ROWS, LANES), jnp.int16, *chunks)


def pack_grads(order, test, own, other):
    rows = test.shape[0] // NY
    return pl.pallas_call(
        grad_kernel,
        out_shape=jax.ShapeDtypeStruct((NY, BLOCKS * rows + SCALE_ROWS, LANES), jnp.int16),
        in_specs=[pl.BlockSpec(memory_space=pltpu.SMEM), VMEM, VMEM, VMEM],
        out_specs=VMEM,
        scratch_shapes=[pltpu.VMEM((test.shape[0], 2 * own.shape[1]), jnp.float32)],
        compiler_params=pltpu.CompilerParams(vmem_limit_bytes=24 << 20),
    )(order, test, own, other)


def on_device(
    train_act, train_grad, train_seg, train_mask, test_act, test_grad, test_seg, test_mask
):
    x, y, c = (lax.axis_index(a) for a in ("x", "y", "c"))
    wide = test_act.shape[1]
    both_z = lax.all_gather(jnp.concatenate([test_act, test_grad], 1), "z", axis=0, tiled=True)
    act_z, grad_z = both_z[:, :wide], both_z[:, wide:]
    other_grad, other_act = swap(train_grad.T, "c"), swap(train_act, "c")
    grads = lax.all_gather(grad_z, "x", axis=0, tiled=True)
    acts = over_x(act_z)

    def grams(chunks, own, other):
        both = jnp.concatenate([own, other], 0)
        return [cross_rows(t, both) for t in chunks]

    order = jnp.stack([(x - step) % NX for step in (0, 1, 3, 2)])
    grad_y = sum_over_y(pack_grads(order, grads, train_grad.T, other_grad))
    act_y = sum_over_y(pack_acts(grams(acts, train_act, other_act)))
    behind = (y // 2) ^ (y // 4)
    local = test_act.shape[0]
    seg, mask = (
        lax.dynamic_slice(
            v.reshape(NX, NZ, NC, local), ((x - behind) % NX, 2 * (y % 2), c, 0), (1, 2, 1, local)
        ).reshape(1, -1)
        for v in (test_seg, test_mask)
    )
    test_onehot = (
        (seg == jnp.arange(TEST_SEQS, dtype=jnp.int32)[:, None]) & (mask != 0)
    ).astype(jnp.float32)
    grad_other, act_other = swap(grad_y, "h"), swap(act_y, "h")
    rows = call(
        joint_kernel,
        (TEST_SEQS, BLOCKS * LANES),
        jnp.float32,
        test_onehot,
        act_y,
        act_other,
        grad_y,
        grad_other,
    )
    n = train_act.shape[0]
    masked = jnp.where(train_mask != 0, train_seg, -1)

    def by_sequence(of, values):
        train_onehot = (of == jnp.arange(SEQ_PACK, dtype=jnp.int32)[:, None]).astype(jnp.float32)
        scores = lax.dot_general(
            train_onehot, values, (((1,), (1,)), ((), ())), precision=lax.Precision.HIGHEST
        )
        return jnp.pad(scores, ((0, 4), (0, LANES - TEST_SEQS)))

    mine, theirs = by_sequence(masked, rows[:, :n]), by_sequence(swap(masked, "c"), rows[:, n:])
    to = jnp.arange(NY * NC)[:, None, None] % NC
    spread = jnp.where(to == c, mine[None], theirs[None])
    got = lax.all_to_all(spread, ("y", "c"), 0, 0, tiled=True)
    scores = jnp.sum(got, 0)[:SEQ_PACK, :TEST_SEQS]
    return scores * (1.0 / (SEG_LEN * math.sqrt(FF * D)))


def solution(mesh):
    fine = Mesh(mesh.devices.reshape(NX, NZ, NC, NY, NH), ("x", "z", "c", "y", "h"))
    return jax.shard_map(
        on_device,
        mesh=fine,
        in_specs=(P(DP, FFN), P(DP, FFN), P(DP, None), P(DP, None), P(DP, FFN), P(DP, FFN), P(), P()),
        out_specs=P(DP, None),
        check_vma=False,
    )
```

```python
import math

import jax
import jax.numpy as jnp
from jax import lax
from jax.experimental import pallas as pl
from jax.experimental.pallas import tpu as pltpu
from jax.sharding import Mesh, PartitionSpec as P

D = 5120
FF = 25600
SEG_LEN = 256
SEQ_PACK = 4
TEST_SEQS = 8
NX, NZ, NC, NY, NH = 4, 4, 2, 8, 2
DP = ("x", "z", "c")
FFN = ("y", "h")
LANES = 128
BLOCKS = 8
SCALE_ROWS = 16
STEPS = 128.0
TOP = 32000.0


def cross_rows(left, right):
    return lax.dot_general(
        left, right, (((1,), (1,)), ((), ())), preferred_element_type=jnp.float32
    )


def swap(value, axis):
    return lax.ppermute(value, axis, [(0, 1), (1, 0)])


ORDER = (1, 3, 2)
REGIONS = ((0, 64), (BLOCKS * 64 + SCALE_ROWS, 16))


def around(value, axis):
    return [value] + [
        lax.ppermute(value, axis, [(i, (i + step) % 4) for i in range(4)]) for step in ORDER
    ]


def step_of(k):
    return k ^ (k // 2)


def pack(parts, out, lead, base=0):
    blocks = parts.blocks
    exponents = []
    for b in range(blocks):
        pieces = parts(b)
        rows = pieces[0].shape[0]
        most = jnp.max(jnp.abs(pieces[0]), axis=0, keepdims=True)
        for p in pieces[1:]:
            most = jnp.maximum(most, jnp.max(jnp.abs(p), axis=0, keepdims=True))
        e = jnp.ceil(jnp.log(jnp.maximum(most, 1e-30)) * STEPS)
        factor = jnp.exp(e * (-1.0 / STEPS)) * TOP
        exponents.append(e)
        for i, p in enumerate(pieces):
            q = jnp.round(p * factor).astype(jnp.int32).astype(jnp.int16)
            out[lead[i] + (slice(base + b * rows, base + (b + 1) * rows), slice(None))] = q
    pad = [jnp.zeros((SCALE_ROWS - blocks, LANES), jnp.float32)]
    tail = jnp.concatenate(exponents + pad, 0).astype(jnp.int32).astype(jnp.int16)
    top = base + blocks * rows
    for at in lead:
        out[at + (slice(top, top + SCALE_ROWS), slice(None))] = tail


class Pieces:
    def __init__(self, blocks, get):
        self.blocks, self.get = blocks, get

    def __call__(self, b):
        return self.get(b)


def factors_of(tail):
    return jnp.exp(tail.astype(jnp.float32) * (1.0 / STEPS)) * (1.0 / TOP)


def pack_kernel(*refs):
    chunks, out = refs[:-1], refs[-1]
    per = chunks[0].shape[0] // NY

    def pieces(b):
        cols = slice(b * LANES, (b + 1) * LANES)
        return [
            jnp.concatenate([r[d * per : (d + 1) * per, cols] for r in chunks], 0) for d in range(NY)
        ]

    pack(Pieces(BLOCKS, pieces), out, [(d,) for d in range(NY)])


def first_kernel(order, test, own, other, act_gram, out, gram):
    n = own.shape[1]
    gram[:, :n] = jnp.dot(test[...], own[...], preferred_element_type=jnp.float32)
    gram[:, n:] = jnp.dot(test[...], other[...], preferred_element_type=jnp.float32)
    height = test.shape[0] // NX
    per = height // NY

    def grads(b):
        cols = slice(b * LANES, (b + 1) * LANES)
        found = []
        for d in range(NY):
            firsts = [pl.multiple_of(order[j] * height + d * per, per) for j in range(NX)]
            found.append(jnp.concatenate([gram[pl.ds(f, per), cols] for f in firsts], 0))
        return found

    def acts(b):
        cols = slice(b * LANES, (b + 1) * LANES)
        return [act_gram[d * per : (d + 1) * per, cols] for d in range(NY)]

    lead = [(d,) for d in range(NY)]
    for (base, _), get in zip(REGIONS, (grads, acts)):
        pack(Pieces(BLOCKS, get), out, lead, base)


def unpack(got, out, base, rows):
    top = base + BLOCKS * rows
    factors = [factors_of(got[s, top : top + SCALE_ROWS, :]) for s in range(NY)]

    def pieces(b):
        total = jnp.zeros((rows, LANES), jnp.float32)
        for s in range(NY):
            block = got[s, base + b * rows : base + (b + 1) * rows, :].astype(jnp.float32)
            total = total + block * factors[s][b : b + 1]
        return [total]

    pack(Pieces(BLOCKS, pieces), out, [()], base)


def unpack_first_kernel(got, out):
    for base, rows in REGIONS:
        unpack(got, out, base, rows)


def unpack_kernel(got, out):
    unpack(got, out, 0, (got.shape[1] - SCALE_ROWS) // BLOCKS)


def joint_kernel(onehot, first_own, first_other, rest_own, rest_other, out):
    def reader(own, other, base, rows):
        top = base + BLOCKS * rows
        f_own = factors_of(own[top : top + SCALE_ROWS, :])
        f_other = factors_of(other[top : top + SCALE_ROWS, :])

        def read(b):
            at = slice(base + b * rows, base + (b + 1) * rows)
            return (
                own[at, :].astype(jnp.float32) * f_own[b : b + 1]
                + other[at, :].astype(jnp.float32) * f_other[b : b + 1]
            )

        return read

    grads = reader(first_own, first_other, *REGIONS[0])
    acts = reader(first_own, first_other, *REGIONS[1])
    rest = reader(rest_own, rest_other, 0, (rest_own.shape[0] - SCALE_ROWS) // BLOCKS)
    for b in range(BLOCKS):
        joint = jnp.concatenate([acts(b), rest(b)], 0) * grads(b)
        out[:, b * LANES : (b + 1) * LANES] = lax.dot_general(
            onehot[...],
            joint,
            (((1,), (0,)), ((), ())),
            precision=lax.Precision.HIGHEST,
            preferred_element_type=jnp.float32,
        )


VMEM = pl.BlockSpec(memory_space=pltpu.VMEM)


def call(kernel, shape, dtype, *args):
    return pl.pallas_call(
        kernel,
        out_shape=jax.ShapeDtypeStruct(shape, dtype),
        in_specs=[VMEM] * len(args),
        out_specs=VMEM,
        compiler_params=pltpu.CompilerParams(vmem_limit_bytes=24 << 20),
    )(*args)


def sum_over_y(packed, kernel):
    got = lax.all_to_all(packed, "y", 0, 0, tiled=True)
    return call(kernel, packed.shape[1:], jnp.int16, got)


def pack_acts(chunks):
    rows = chunks[0].shape[0] * len(chunks) // NY
    return call(pack_kernel, (NY, BLOCKS * rows + SCALE_ROWS, LANES), jnp.int16, *chunks)


def pack_first(order, test, own, other, act_gram):
    base, rows = REGIONS[1]
    return pl.pallas_call(
        first_kernel,
        out_shape=jax.ShapeDtypeStruct((NY, base + BLOCKS * rows + SCALE_ROWS, LANES), jnp.int16),
        in_specs=[pl.BlockSpec(memory_space=pltpu.SMEM)] + [VMEM] * 4,
        out_specs=VMEM,
        scratch_shapes=[pltpu.VMEM((test.shape[0], 2 * own.shape[1]), jnp.float32)],
        compiler_params=pltpu.CompilerParams(vmem_limit_bytes=24 << 20),
    )(order, test, own, other, act_gram)


def on_device(
    train_act, train_grad, train_seg, train_mask, test_act, test_grad, test_seg, test_mask
):
    x, y, z, c = (lax.axis_index(a) for a in ("x", "y", "z", "c"))
    wide = test_act.shape[1]
    both_z = jnp.concatenate(around(jnp.concatenate([test_act, test_grad], 1), "z"), 0)
    act_z, grad_z = both_z[:, :wide], both_z[:, wide:]
    other_grad, other_act = swap(train_grad.T, "c"), swap(train_act, "c")
    grads = lax.all_gather(grad_z, "x", axis=0, tiled=True)
    acts = around(act_z, "x")
    both = jnp.concatenate([train_act, other_act], 0)
    grams = [cross_rows(t, both) for t in acts]
    order = jnp.stack([(x - step) % NX for step in (0,) + ORDER])
    first = sum_over_y(
        pack_first(order, grads, train_grad.T, other_grad, grams[0]), unpack_first_kernel
    )
    rest = sum_over_y(pack_acts(grams[1:]), unpack_kernel)
    local = test_act.shape[0]
    per = NZ * local // NY
    from_z, from_row = (z - step_of(y * per // local)) % NZ, y * per % local

    def here(values):
        cut = lax.dynamic_slice(
            values.reshape(NX, NZ, NC, local), (0, from_z, c, from_row), (NX, 1, 1, per)
        ).reshape(NX, per)
        return jnp.concatenate(
            [
                jnp.sum(jnp.where(jnp.arange(NX)[:, None] == (x - s) % NX, cut, 0), 0, keepdims=True)
                for s in (0,) + ORDER
            ],
            1,
        )

    test_onehot = (
        (here(test_seg) == jnp.arange(TEST_SEQS, dtype=jnp.int32)[:, None]) & (here(test_mask) != 0)
    ).astype(jnp.float32)
    rows = call(
        joint_kernel,
        (TEST_SEQS, BLOCKS * LANES),
        jnp.float32,
        test_onehot,
        first,
        swap(first, "h"),
        rest,
        swap(rest, "h"),
    )
    n = train_act.shape[0]
    masked = jnp.where(train_mask != 0, train_seg, -1)

    def by_sequence(of, values):
        train_onehot = (of == jnp.arange(SEQ_PACK, dtype=jnp.int32)[:, None]).astype(jnp.float32)
        scores = lax.dot_general(
            train_onehot, values, (((1,), (1,)), ((), ())), precision=lax.Precision.HIGHEST
        )
        return jnp.pad(scores, ((0, 4), (0, LANES - TEST_SEQS)))

    mine, theirs = by_sequence(masked, rows[:, :n]), by_sequence(swap(masked, "c"), rows[:, n:])
    to = jnp.arange(NY * NC)[:, None, None] % NC
    spread = jnp.where(to == c, mine[None], theirs[None])
    got = lax.all_to_all(spread, ("y", "c"), 0, 0, tiled=True)
    scores = jnp.sum(got, 0)[:SEQ_PACK, :TEST_SEQS]
    return scores * (1.0 / (SEG_LEN * math.sqrt(FF * D)))


def solution(mesh):
    fine = Mesh(mesh.devices.reshape(NX, NZ, NC, NY, NH), ("x", "z", "c", "y", "h"))
    return jax.shard_map(
        on_device,
        mesh=fine,
        in_specs=(P(DP, FFN), P(DP, FFN), P(DP, None), P(DP, None), P(DP, FFN), P(DP, FFN), P(), P()),
        out_specs=P(DP, None),
        check_vma=False,
    )
```

```python
import math

import jax
import jax.numpy as jnp
from jax import lax
from jax.experimental import pallas as pl
from jax.experimental.pallas import tpu as pltpu
from jax.sharding import Mesh, PartitionSpec as P

D = 5120
FF = 25600
SEG_LEN = 256
SEQ_PACK = 4
TEST_SEQS = 8
NX, NZ, NC, NY, NH = 4, 4, 2, 8, 2
DP = ("x", "z", "c")
FFN = ("y", "h")
LANES = 128
BLOCKS = 8
SCALE_ROWS = 16
STEPS = 128.0
TOP = 32000.0


def cross_rows(left, right):
    return lax.dot_general(
        left, right, (((1,), (1,)), ((), ())), preferred_element_type=jnp.float32
    )


def swap(value, axis):
    return lax.ppermute(value, axis, [(0, 1), (1, 0)])


def over_x(value):
    return [value] + [
        lax.ppermute(value, "x", [(i, (i + step) % NX) for i in range(NX)]) for step in (1, 3, 2)
    ]


def pack(parts, out, lead):
    blocks = parts.blocks
    exponents = []
    for b in range(blocks):
        pieces = parts(b)
        rows = pieces[0].shape[0]
        most = jnp.max(jnp.abs(pieces[0]), axis=0, keepdims=True)
        for p in pieces[1:]:
            most = jnp.maximum(most, jnp.max(jnp.abs(p), axis=0, keepdims=True))
        e = jnp.ceil(jnp.log(jnp.maximum(most, 1e-30)) * STEPS)
        factor = jnp.exp(e * (-1.0 / STEPS)) * TOP
        exponents.append(e)
        for i, p in enumerate(pieces):
            q = jnp.round(p * factor).astype(jnp.int32).astype(jnp.int16)
            out[lead[i] + (slice(b * rows, (b + 1) * rows), slice(None))] = q
    pad = [jnp.zeros((SCALE_ROWS - blocks, LANES), jnp.float32)]
    tail = jnp.concatenate(exponents + pad, 0).astype(jnp.int32).astype(jnp.int16)
    for at in lead:
        out[at + (slice(blocks * rows, blocks * rows + SCALE_ROWS), slice(None))] = tail


class Pieces:
    def __init__(self, blocks, get):
        self.blocks, self.get = blocks, get

    def __call__(self, b):
        return self.get(b)


def factors_of(tail):
    return jnp.exp(tail.astype(jnp.float32) * (1.0 / STEPS)) * (1.0 / TOP)


def pack_kernel(*refs):
    chunks, out = refs[:-1], refs[-1]
    rows = chunks[0].shape[0] * len(chunks) // NY
    per = chunks[0].shape[0] // rows

    def pieces(b):
        cols = slice(b * LANES, (b + 1) * LANES)
        return [
            chunks[d // per][(d % per) * rows : (d % per + 1) * rows, cols] for d in range(NY)
        ]

    pack(Pieces(chunks[0].shape[1] // LANES, pieces), out, [(d,) for d in range(NY)])


def grad_kernel(order, test, own, other, out, gram):
    n = own.shape[1]
    gram[:, :n] = jnp.dot(test[...], own[...], preferred_element_type=jnp.float32)
    gram[:, n:] = jnp.dot(test[...], other[...], preferred_element_type=jnp.float32)
    height = test.shape[0] // NX
    rows = test.shape[0] // NY
    per = height // rows

    def pieces(b):
        cols = slice(b * LANES, (b + 1) * LANES)
        found = []
        for d in range(NY):
            first = pl.multiple_of(order[d // per] * height + (d % per) * rows, rows)
            found.append(gram[pl.ds(first, rows), cols])
        return found

    pack(Pieces(2 * n // LANES, pieces), out, [(d,) for d in range(NY)])


def unpack_kernel(got, out):
    blocks = BLOCKS
    rows = (got.shape[1] - SCALE_ROWS) // blocks
    factors = [factors_of(got[s, blocks * rows :, :]) for s in range(NY)]

    def pieces(b):
        total = jnp.zeros((rows, LANES), jnp.float32)
        for s in range(NY):
            block = got[s, b * rows : (b + 1) * rows, :].astype(jnp.float32)
            total = total + block * factors[s][b : b + 1]
        return [total]

    pack(Pieces(blocks, pieces), out, [()])


def joint_kernel(onehot, act_own, act_other, grad_own, grad_other, out):
    blocks = BLOCKS
    rows = (act_own.shape[0] - SCALE_ROWS) // blocks

    def part(ref, factor, b):
        return ref[b * rows : (b + 1) * rows, :].astype(jnp.float32) * factor[b : b + 1]

    refs = (act_own, act_other, grad_own, grad_other)
    f = [factors_of(r[blocks * rows :, :]) for r in refs]
    for b in range(blocks):
        a0, a1, g0, g1 = (part(r, k, b) for r, k in zip(refs, f))
        joint = (a0 + a1) * (g0 + g1)
        out[:, b * LANES : (b + 1) * LANES] = lax.dot_general(
            onehot[...],
            joint,
            (((1,), (0,)), ((), ())),
            precision=lax.Precision.HIGHEST,
            preferred_element_type=jnp.float32,
        )


VMEM = pl.BlockSpec(memory_space=pltpu.VMEM)


def call(kernel, shape, dtype, *args):
    return pl.pallas_call(
        kernel,
        out_shape=jax.ShapeDtypeStruct(shape, dtype),
        in_specs=[VMEM] * len(args),
        out_specs=VMEM,
        compiler_params=pltpu.CompilerParams(vmem_limit_bytes=24 << 20),
    )(*args)


def sum_over_y(packed):
    got = lax.all_to_all(packed, "y", 0, 0, tiled=True)
    return call(unpack_kernel, packed.shape[1:], jnp.int16, got)


def pack_acts(chunks):
    rows = chunks[0].shape[0] * len(chunks) // NY
    return call(pack_kernel, (NY, BLOCKS * rows + SCALE_ROWS, LANES), jnp.int16, *chunks)


def pack_grads(order, test, own, other):
    rows = test.shape[0] // NY
    return pl.pallas_call(
        grad_kernel,
        out_shape=jax.ShapeDtypeStruct((NY, BLOCKS * rows + SCALE_ROWS, LANES), jnp.int16),
        in_specs=[pl.BlockSpec(memory_space=pltpu.SMEM), VMEM, VMEM, VMEM],
        out_specs=VMEM,
        scratch_shapes=[pltpu.VMEM((test.shape[0], 2 * own.shape[1]), jnp.float32)],
        compiler_params=pltpu.CompilerParams(vmem_limit_bytes=24 << 20),
    )(order, test, own, other)


def on_device(
    train_act, train_grad, train_seg, train_mask, test_act, test_grad, test_seg, test_mask
):
    x, y, c = (lax.axis_index(a) for a in ("x", "y", "c"))
    wide = test_act.shape[1]
    both_z = lax.all_gather(jnp.concatenate([test_act, test_grad], 1), "z", axis=0, tiled=True)
    act_z, grad_z = both_z[:, :wide], both_z[:, wide:]
    other_grad, other_act = swap(train_grad.T, "c"), swap(train_act, "c")
    grads = lax.all_gather(grad_z, "x", axis=0, tiled=True)
    acts = over_x(act_z)

    def grams(chunks, own, other):
        both = jnp.concatenate([own, other], 0)
        return [cross_rows(t, both) for t in chunks]

    order = jnp.stack([(x - step) % NX for step in (0, 1, 3, 2)])
    grad_y = sum_over_y(pack_grads(order, grads, train_grad.T, other_grad))
    act_y = sum_over_y(pack_acts(grams(acts, train_act, other_act)))
    behind = (y // 2) ^ (y // 4)
    local = test_act.shape[0]
    seg, mask = (
        lax.dynamic_slice(
            v.reshape(NX, NZ, NC, local), ((x - behind) % NX, 2 * (y % 2), c, 0), (1, 2, 1, local)
        ).reshape(1, -1)
        for v in (test_seg, test_mask)
    )
    test_onehot = (
        (seg == jnp.arange(TEST_SEQS, dtype=jnp.int32)[:, None]) & (mask != 0)
    ).astype(jnp.float32)
    grad_pair = lax.all_gather(grad_y, "h")
    grad_y, grad_other = grad_pair[0], grad_pair[1]
    act_pair = lax.all_gather(act_y, "h")
    act_y, act_other = act_pair[0], act_pair[1]
    rows = call(
        joint_kernel,
        (TEST_SEQS, BLOCKS * LANES),
        jnp.float32,
        test_onehot,
        act_y,
        act_other,
        grad_y,
        grad_other,
    )
    n = train_act.shape[0]
    masked = jnp.where(train_mask != 0, train_seg, -1)

    def by_sequence(of, values):
        train_onehot = (of == jnp.arange(SEQ_PACK, dtype=jnp.int32)[:, None]).astype(jnp.float32)
        scores = lax.dot_general(
            train_onehot, values, (((1,), (1,)), ((), ())), precision=lax.Precision.HIGHEST
        )
        return jnp.pad(scores, ((0, 4), (0, LANES - TEST_SEQS)))

    mine, theirs = by_sequence(masked, rows[:, :n]), by_sequence(swap(masked, "c"), rows[:, n:])
    to = jnp.arange(NY * NC)[:, None, None] % NC
    spread = jnp.where(to == c, mine[None], theirs[None])
    got = lax.all_to_all(spread, ("y", "c"), 0, 0, tiled=True)
    scores = jnp.sum(got, 0)[:SEQ_PACK, :TEST_SEQS]
    return scores * (1.0 / (SEG_LEN * math.sqrt(FF * D)))


def solution(mesh):
    fine = Mesh(mesh.devices.reshape(NX, NZ, NC, NY, NH), ("x", "z", "c", "y", "h"))
    return jax.shard_map(
        on_device,
        mesh=fine,
        in_specs=(P(DP, FFN), P(DP, FFN), P(DP, None), P(DP, None), P(DP, FFN), P(DP, FFN), P(), P()),
        out_specs=P(DP, None),
        check_vma=False,
    )
```

```python
import math

import jax
import jax.numpy as jnp
from jax import lax
from jax.experimental import pallas as pl
from jax.experimental.pallas import tpu as pltpu
from jax.sharding import Mesh, PartitionSpec as P

D = 5120
FF = 25600
SEG_LEN = 256
SEQ_PACK = 4
TEST_SEQS = 8
NX, NZ, NC, NY, NH = 4, 4, 2, 8, 2
DP = ("x", "z", "c")
FFN = ("y", "h")
LANES = 128
BLOCKS = 8
SCALE_ROWS = 16
STEPS = 128.0
TOP = 32000.0


def cross_rows(left, right):
    return lax.dot_general(
        left, right, (((1,), (1,)), ((), ())), preferred_element_type=jnp.float32
    )


def swap(value, axis):
    return lax.ppermute(value, axis, [(0, 1), (1, 0)])


def over_x(value):
    return [value] + [
        lax.ppermute(value, "x", [(i, (i + step) % NX) for i in range(NX)]) for step in (1, 3, 2)
    ]


def pack(parts, out, lead):
    blocks = parts.blocks
    exponents = []
    for b in range(blocks):
        pieces = parts(b)
        rows = pieces[0].shape[0]
        most = jnp.max(jnp.abs(pieces[0]), axis=0, keepdims=True)
        for p in pieces[1:]:
            most = jnp.maximum(most, jnp.max(jnp.abs(p), axis=0, keepdims=True))
        e = jnp.ceil(jnp.log(jnp.maximum(most, 1e-30)) * STEPS)
        factor = jnp.exp(e * (-1.0 / STEPS)) * TOP
        exponents.append(e)
        for i, p in enumerate(pieces):
            q = jnp.round(p * factor).astype(jnp.int32).astype(jnp.int16)
            out[lead[i] + (slice(b * rows, (b + 1) * rows), slice(None))] = q
    pad = [jnp.zeros((SCALE_ROWS - blocks, LANES), jnp.float32)]
    tail = jnp.concatenate(exponents + pad, 0).astype(jnp.int32).astype(jnp.int16)
    for at in lead:
        out[at + (slice(blocks * rows, blocks * rows + SCALE_ROWS), slice(None))] = tail


class Pieces:
    def __init__(self, blocks, get):
        self.blocks, self.get = blocks, get

    def __call__(self, b):
        return self.get(b)


def factors_of(tail):
    return jnp.exp(tail.astype(jnp.float32) * (1.0 / STEPS)) * (1.0 / TOP)


def grad_kernel(order, test, own, other, out, gram):
    n = own.shape[1]
    gram[:, :n] = jnp.dot(test[...], own[...], preferred_element_type=jnp.float32)
    gram[:, n:] = jnp.dot(test[...], other[...], preferred_element_type=jnp.float32)
    height = test.shape[0] // NX
    rows = test.shape[0] // NY
    per = height // rows

    def pieces(b):
        cols = slice(b * LANES, (b + 1) * LANES)
        found = []
        for d in range(NY):
            first = pl.multiple_of(order[d // per] * height + (d % per) * rows, rows)
            found.append(gram[pl.ds(first, rows), cols])
        return found

    pack(Pieces(2 * n // LANES, pieces), out, [(d,) for d in range(NY)])


def unpack_kernel(got, out):
    blocks = BLOCKS
    rows = (got.shape[1] - SCALE_ROWS) // blocks
    factors = [factors_of(got[s, blocks * rows :, :]) for s in range(NY)]

    def pieces(b):
        total = jnp.zeros((rows, LANES), jnp.float32)
        for s in range(NY):
            block = got[s, b * rows : (b + 1) * rows, :].astype(jnp.float32)
            total = total + block * factors[s][b : b + 1]
        return [total]

    pack(Pieces(blocks, pieces), out, [()])


def both_kernel(pair, out):
    rows = (pair.shape[1] - SCALE_ROWS) // BLOCKS
    factors = [factors_of(pair[i, BLOCKS * rows :, :]) for i in range(NH)]

    def pieces(b):
        at = slice(b * rows, (b + 1) * rows)
        low, high = (
            pair[i, at, :].astype(jnp.float32) * factors[i][b : b + 1] for i in range(NH)
        )
        return [low + high]

    pack(Pieces(BLOCKS, pieces), out, [()])


def joint_kernel(onehot, grads, *refs):
    chunks, out = refs[:-1], refs[-1]
    rows = (grads.shape[1] - SCALE_ROWS) // BLOCKS
    per = chunks[0].shape[0] // rows
    factors = [factors_of(grads[d, BLOCKS * rows :, :]) for d in range(NY)]
    for b in range(BLOCKS):
        cols = slice(b * LANES, (b + 1) * LANES)
        parts = []
        for d in range(NY):
            grad = grads[d, b * rows : (b + 1) * rows, :].astype(jnp.float32) * factors[d][b : b + 1]
            parts.append(chunks[d // per][(d % per) * rows : (d % per + 1) * rows, cols] * grad)
        out[:, cols] = lax.dot_general(
            onehot[...],
            jnp.concatenate(parts, 0),
            (((1,), (0,)), ((), ())),
            precision=lax.Precision.HIGHEST,
            preferred_element_type=jnp.float32,
        )


VMEM = pl.BlockSpec(memory_space=pltpu.VMEM)


def call(kernel, shape, dtype, *args):
    return pl.pallas_call(
        kernel,
        out_shape=jax.ShapeDtypeStruct(shape, dtype),
        in_specs=[VMEM] * len(args),
        out_specs=VMEM,
        compiler_params=pltpu.CompilerParams(vmem_limit_bytes=24 << 20),
    )(*args)


def sum_over_y(packed):
    got = lax.all_to_all(packed, "y", 0, 0, tiled=True)
    return call(unpack_kernel, packed.shape[1:], jnp.int16, got)


def pack_grads(order, test, own, other):
    rows = test.shape[0] // NY
    return pl.pallas_call(
        grad_kernel,
        out_shape=jax.ShapeDtypeStruct((NY, BLOCKS * rows + SCALE_ROWS, LANES), jnp.int16),
        in_specs=[pl.BlockSpec(memory_space=pltpu.SMEM), VMEM, VMEM, VMEM],
        out_specs=VMEM,
        scratch_shapes=[pltpu.VMEM((test.shape[0], 2 * own.shape[1]), jnp.float32)],
        compiler_params=pltpu.CompilerParams(vmem_limit_bytes=24 << 20),
    )(order, test, own, other)


def on_device(
    train_act, train_grad, train_seg, train_mask, test_act, test_grad, test_seg, test_mask
):
    x, y, c = (lax.axis_index(a) for a in ("x", "y", "c"))
    wide = test_act.shape[1]
    both_z = lax.all_gather(jnp.concatenate([test_act, test_grad], 1), "z", axis=0, tiled=True)
    act_z, grad_z = both_z[:, :wide], both_z[:, wide:]
    other_grad, other_act = swap(train_grad.T, "c"), swap(train_act, "c")
    grads = lax.all_gather(grad_z, "x", axis=0, tiled=True)
    acts = over_x(act_z)

    def grams(chunks, own, other):
        both = jnp.concatenate([own, other], 0)
        return [cross_rows(t, both) for t in chunks]

    order = jnp.stack([(x - step) % NX for step in (0, 1, 3, 2)])
    grad_y = sum_over_y(pack_grads(order, grads, train_grad.T, other_grad))
    pair = lax.all_gather(grad_y, "h")
    grad_all = lax.all_gather(call(both_kernel, grad_y.shape, jnp.int16, pair), "y")
    chunks = grams(acts, train_act, other_act)
    local = test_act.shape[0]

    def here(values):
        cut = lax.dynamic_slice(
            values.reshape(NX, NZ, NC, local), (0, 0, c, 0), (NX, NZ, 1, local)
        ).reshape(NX, NZ * local)
        return jnp.concatenate(
            [
                jnp.sum(jnp.where(jnp.arange(NX)[:, None] == (x - s) % NX, cut, 0), 0, keepdims=True)
                for s in (0, 1, 3, 2)
            ],
            1,
        )

    test_onehot = (
        (here(test_seg) == jnp.arange(TEST_SEQS, dtype=jnp.int32)[:, None]) & (here(test_mask) != 0)
    ).astype(jnp.float32)
    rows = call(
        joint_kernel, (TEST_SEQS, BLOCKS * LANES), jnp.float32, test_onehot, grad_all, *chunks
    )
    n = train_act.shape[0]
    masked = jnp.where(train_mask != 0, train_seg, -1)

    def by_sequence(of, values):
        train_onehot = (of == jnp.arange(SEQ_PACK, dtype=jnp.int32)[:, None]).astype(jnp.float32)
        scores = lax.dot_general(
            train_onehot, values, (((1,), (1,)), ((), ())), precision=lax.Precision.HIGHEST
        )
        return jnp.pad(scores, ((0, 4), (0, LANES - TEST_SEQS)))

    mine, theirs = by_sequence(masked, rows[:, :n]), by_sequence(swap(masked, "c"), rows[:, n:])
    to = jnp.arange(NY * NC)[:, None, None] % NC
    spread = jnp.where(to == c, mine[None], theirs[None])
    got = lax.all_to_all(spread, ("y", "c"), 0, 0, tiled=True)
    scores = jnp.sum(got, 0)
    scores = (scores + swap(scores, "h"))[:SEQ_PACK, :TEST_SEQS]
    return scores * (1.0 / (SEG_LEN * math.sqrt(FF * D)))


def solution(mesh):
    fine = Mesh(mesh.devices.reshape(NX, NZ, NC, NY, NH), ("x", "z", "c", "y", "h"))
    return jax.shard_map(
        on_device,
        mesh=fine,
        in_specs=(P(DP, FFN), P(DP, FFN), P(DP, None), P(DP, None), P(DP, FFN), P(DP, FFN), P(), P()),
        out_specs=P(DP, None),
        check_vma=False,
    )
```

```python
import math

import jax
import jax.numpy as jnp
from jax import lax
from jax.experimental import pallas as pl
from jax.experimental.pallas import tpu as pltpu
from jax.sharding import Mesh, PartitionSpec as P

D = 5120
FF = 25600
SEG_LEN = 256
SEQ_PACK = 4
TEST_SEQS = 8
NX, NZ, NC, NY, NH = 4, 4, 2, 8, 2
DP = ("x", "z", "c")
FFN = ("y", "h")
LANES = 128
BLOCKS = 8
SCALE_ROWS = 16
STEPS = 128.0
TOP = 32000.0


def cross_rows(left, right):
    return lax.dot_general(
        left, right, (((1,), (1,)), ((), ())), preferred_element_type=jnp.float32
    )


def swap(value, axis):
    return lax.ppermute(value, axis, [(0, 1), (1, 0)])


def over_x(value):
    return [value] + [
        lax.ppermute(value, "x", [(i, (i + step) % NX) for i in range(NX)]) for step in (1, 3, 2)
    ]


def pack(parts, out, lead):
    blocks = parts.blocks
    exponents = []
    for b in range(blocks):
        pieces = parts(b)
        rows = pieces[0].shape[0]
        most = jnp.max(jnp.abs(pieces[0]), axis=0, keepdims=True)
        for p in pieces[1:]:
            most = jnp.maximum(most, jnp.max(jnp.abs(p), axis=0, keepdims=True))
        e = jnp.ceil(jnp.log(jnp.maximum(most, 1e-30)) * STEPS)
        factor = jnp.exp(e * (-1.0 / STEPS)) * TOP
        exponents.append(e)
        for i, p in enumerate(pieces):
            q = jnp.round(p * factor).astype(jnp.int32).astype(jnp.int16)
            out[lead[i] + (slice(b * rows, (b + 1) * rows), slice(None))] = q
    pad = [jnp.zeros((SCALE_ROWS - blocks, LANES), jnp.float32)]
    tail = jnp.concatenate(exponents + pad, 0).astype(jnp.int32).astype(jnp.int16)
    for at in lead:
        out[at + (slice(blocks * rows, blocks * rows + SCALE_ROWS), slice(None))] = tail


class Pieces:
    def __init__(self, blocks, get):
        self.blocks, self.get = blocks, get

    def __call__(self, b):
        return self.get(b)


def factors_of(tail):
    return jnp.exp(tail.astype(jnp.float32) * (1.0 / STEPS)) * (1.0 / TOP)


def pack_kernel(*refs):
    chunks, out = refs[:-1], refs[-1]
    rows = chunks[0].shape[0] * len(chunks) // NY
    per = chunks[0].shape[0] // rows

    def pieces(b):
        cols = slice(b * LANES, (b + 1) * LANES)
        return [
            chunks[d // per][(d % per) * rows : (d % per + 1) * rows, cols] for d in range(NY)
        ]

    pack(Pieces(chunks[0].shape[1] // LANES, pieces), out, [(d,) for d in range(NY)])


def grad_kernel(order, test, own, other, out, gram):
    n = own.shape[1]
    gram[:, :n] = jnp.dot(test[...], own[...], preferred_element_type=jnp.float32)
    gram[:, n:] = jnp.dot(test[...], other[...], preferred_element_type=jnp.float32)
    height = test.shape[0] // NX
    rows = test.shape[0] // NY
    per = height // rows

    def pieces(b):
        cols = slice(b * LANES, (b + 1) * LANES)
        found = []
        for d in range(NY):
            first = pl.multiple_of(order[d // per] * height + (d % per) * rows, rows)
            found.append(gram[pl.ds(first, rows), cols])
        return found

    pack(Pieces(2 * n // LANES, pieces), out, [(d,) for d in range(NY)])


def unpack_kernel(got, out):
    blocks = BLOCKS
    rows = (got.shape[1] - SCALE_ROWS) // blocks
    factors = [factors_of(got[s, blocks * rows :, :]) for s in range(NY)]

    def pieces(b):
        total = jnp.zeros((rows, LANES), jnp.float32)
        for s in range(NY):
            block = got[s, b * rows : (b + 1) * rows, :].astype(jnp.float32)
            total = total + block * factors[s][b : b + 1]
        return [total]

    pack(Pieces(blocks, pieces), out, [()])


def joint_kernel(onehot, act_own, grad_own, grad_other, out):
    blocks = BLOCKS
    rows = (act_own.shape[0] - SCALE_ROWS) // blocks

    def part(ref, factor, b):
        return ref[b * rows : (b + 1) * rows, :].astype(jnp.float32) * factor[b : b + 1]

    refs = (act_own, grad_own, grad_other)
    f = [factors_of(r[blocks * rows :, :]) for r in refs]
    for b in range(blocks):
        act, g0, g1 = (part(r, k, b) for r, k in zip(refs, f))
        joint = act * (g0 + g1)
        out[:, b * LANES : (b + 1) * LANES] = lax.dot_general(
            onehot[...],
            joint,
            (((1,), (0,)), ((), ())),
            precision=lax.Precision.HIGHEST,
            preferred_element_type=jnp.float32,
        )


VMEM = pl.BlockSpec(memory_space=pltpu.VMEM)


def call(kernel, shape, dtype, *args):
    return pl.pallas_call(
        kernel,
        out_shape=jax.ShapeDtypeStruct(shape, dtype),
        in_specs=[VMEM] * len(args),
        out_specs=VMEM,
        compiler_params=pltpu.CompilerParams(vmem_limit_bytes=24 << 20),
    )(*args)


def sum_over_y(packed):
    got = lax.all_to_all(packed, "y", 0, 0, tiled=True)
    return call(unpack_kernel, packed.shape[1:], jnp.int16, got)


def pack_acts(chunks):
    rows = chunks[0].shape[0] * len(chunks) // NY
    return call(pack_kernel, (NY, BLOCKS * rows + SCALE_ROWS, LANES), jnp.int16, *chunks)


def pack_grads(order, test, own, other):
    rows = test.shape[0] // NY
    return pl.pallas_call(
        grad_kernel,
        out_shape=jax.ShapeDtypeStruct((NY, BLOCKS * rows + SCALE_ROWS, LANES), jnp.int16),
        in_specs=[pl.BlockSpec(memory_space=pltpu.SMEM), VMEM, VMEM, VMEM],
        out_specs=VMEM,
        scratch_shapes=[pltpu.VMEM((test.shape[0], 2 * own.shape[1]), jnp.float32)],
        compiler_params=pltpu.CompilerParams(vmem_limit_bytes=24 << 20),
    )(order, test, own, other)


def on_device(
    train_act, train_grad, train_seg, train_mask, test_act, test_grad, test_seg, test_mask
):
    x, y, c = (lax.axis_index(a) for a in ("x", "y", "c"))
    wide = test_act.shape[1]
    both_z = lax.all_gather(jnp.concatenate([test_act, test_grad], 1), "z", axis=0, tiled=True)
    act_z, grad_z = both_z[:, :wide], both_z[:, wide:]
    other_grad, other_act = swap(train_grad.T, "c"), swap(train_act, "c")
    grads = lax.all_gather(grad_z, "x", axis=0, tiled=True)
    acts = over_x(act_z)

    def grams(chunks, own, other):
        both = jnp.concatenate([own, other], 0)
        return [cross_rows(t, both) for t in chunks]

    order = jnp.stack([(x - step) % NX for step in (0, 1, 3, 2)])
    grad_y = sum_over_y(pack_grads(order, grads, train_grad.T, other_grad))
    act_y = sum_over_y(pack_acts(grams(acts, train_act, other_act)))
    behind = (y // 2) ^ (y // 4)
    local = test_act.shape[0]
    seg, mask = (
        lax.dynamic_slice(
            v.reshape(NX, NZ, NC, local), ((x - behind) % NX, 2 * (y % 2), c, 0), (1, 2, 1, local)
        ).reshape(1, -1)
        for v in (test_seg, test_mask)
    )
    test_onehot = (
        (seg == jnp.arange(TEST_SEQS, dtype=jnp.int32)[:, None]) & (mask != 0)
    ).astype(jnp.float32)
    grad_pair = lax.all_gather(grad_y, "h")
    grad_y, grad_other = grad_pair[0], grad_pair[1]
    rows = call(
        joint_kernel,
        (TEST_SEQS, BLOCKS * LANES),
        jnp.float32,
        test_onehot,
        act_y,
        grad_y,
        grad_other,
    )
    n = train_act.shape[0]
    masked = jnp.where(train_mask != 0, train_seg, -1)

    def by_sequence(of, values):
        train_onehot = (of == jnp.arange(SEQ_PACK, dtype=jnp.int32)[:, None]).astype(jnp.float32)
        scores = lax.dot_general(
            train_onehot, values, (((1,), (1,)), ((), ())), precision=lax.Precision.HIGHEST
        )
        return jnp.pad(scores, ((0, 4), (0, LANES - TEST_SEQS)))

    mine, theirs = by_sequence(masked, rows[:, :n]), by_sequence(swap(masked, "c"), rows[:, n:])
    to = jnp.arange(NY * NC)[:, None, None] % NC
    spread = jnp.where(to == c, mine[None], theirs[None])
    got = lax.all_to_all(spread, ("y", "c"), 0, 0, tiled=True)
    scores = lax.psum(jnp.sum(got, 0), "h")[:SEQ_PACK, :TEST_SEQS]
    return scores * (1.0 / (SEG_LEN * math.sqrt(FF * D)))


def solution(mesh):
    fine = Mesh(mesh.devices.reshape(NX, NZ, NC, NY, NH), ("x", "z", "c", "y", "h"))
    return jax.shard_map(
        on_device,
        mesh=fine,
        in_specs=(P(DP, FFN), P(DP, FFN), P(DP, None), P(DP, None), P(DP, FFN), P(DP, FFN), P(), P()),
        out_specs=P(DP, None),
        check_vma=False,
    )
```
